32 devices in a mesh: gy: 8 (over z, x), gz: 4 (over y, core).
Axes of the slice: x: 2, y: 2, z: 4, core: 2. Of those that a mesh axis runs over, the one named last changes fastest.
Arguments:
- species_field: float32 [256, 256, 256], P('gy', 'gz'), may hold values from -10 to 10
- reaction_source: float32 [256, 256, 256], P('gy', 'gz'), may hold values from -1500 to 1500
- interface_mask: int32 [256, 256, 256], P('gy', 'gz'), may hold values 0 or 1
- phase_labels: int32 [256, 256, 256], P('gy', 'gz'), may hold values from 0 to 3
- phase_diffusivity: float32 [4], replicated, may hold values from 1 to 16
Outputs:
- updated_field: float32 [256, 256, 256], P('gy', 'gz')
The draws below stay inside these ranges and needn't reach their ends.
All inputs are finite; a program needn't handle non-finite values. No bound on the sum of `interface_mask` on one device may be relied on, other than what follows from the above.
Results may differ from the reference program's by a relative error of at most 0.0003.
Values sent between devices are 32-bit elements; how exact they have to be, the bound alone decides.
A program may use at most 128 MiB of HBM per device.

```python
import math
import jax
import jax.numpy as jnp
from jax import lax

NX = 256
NU = 400
PHASES = 4
NY = 256
NZ = 256


def draw_species_field(key, part):
    key = jax.random.fold_in(key, 5)
    subkeys = jax.random.split(key, 3)
    grid_y = ((jnp.arange(NY, dtype=jnp.float32) + 0.5) / NY)[:, None, None]
    grid_z = ((jnp.arange(NZ, dtype=jnp.float32) + 0.5) / NZ)[None, :, None]
    grid_x = ((jnp.arange(NX, dtype=jnp.float32) + 0.5) / NX)[None, None, :]
    rough_part = 0.5 * jnp.clip(jax.random.normal(subkeys[0], (NY, NZ, NX), jnp.float32), -6.0, 6.0)
    amplitude = jax.random.uniform(subkeys[1], (3,), jnp.float32, 0.5, 1.5)
    offsets = jax.random.uniform(subkeys[2], (2,), jnp.float32, 0.0, 2.0 * math.pi)
    across_x = jnp.sin(math.pi * grid_x)
    smooth = amplitude[0] * jnp.sin(math.pi * grid_y) * jnp.sin(math.pi * grid_z) * across_x
    smooth = smooth + amplitude[1] * jnp.sin(2.0 * math.pi * grid_y + offsets[0]) * across_x
    smooth = smooth + amplitude[2] * jnp.sin(2.0 * math.pi * grid_z + offsets[1]) * across_x
    return rough_part + smooth


def draw_reaction_source(key, part):
    key = jax.random.fold_in(key, 7)
    subkeys = jax.random.split(key, 1)
    return 300.0 * jnp.clip(jax.random.normal(subkeys[0], (NY, NZ, NX), jnp.float32), -5.0, 5.0)


def with_ends(array, rng, low, largest):
    dims = array.shape
    index_at = [jax.random.randint(jax.random.fold_in(rng, axis), (), 0, dims[axis]) for axis in range(len(dims))]
    array = array.at[tuple(index_at)].set(low)
    longest = dims.index(max(dims))
    index_at[longest] = (index_at[longest] + 1) % dims[longest]
    return array.at[tuple(index_at)].set(largest)


def setup_inputs(seed: int = 0) -> dict:
    keys = jax.random.split(jax.random.key(seed), 6)
    species_field = draw_species_field(jax.random.fold_in(keys[5], 71), 0)
    reaction_source = draw_reaction_source(jax.random.fold_in(keys[5], 71), 0)
    interface_mask = with_ends((jax.random.randint(keys[2], (NY, NZ, NX), 0, 4) < 1).astype(jnp.int32), jax.random.fold_in(keys[2], 1), 0, 1)
    phase_labels = with_ends(jax.random.randint(keys[3], (NY, NZ, NX), 0, PHASES), jax.random.fold_in(keys[3], 1), 0, PHASES - 1).astype(jnp.int32)
    phase_diffusivity = jnp.clip(jnp.exp(jax.random.uniform(keys[4], (PHASES,), jnp.float32, math.log(1.0), math.log(16.0))), 1.0, 16.0)
    return dict(species_field=species_field, reaction_source=reaction_source, interface_mask=interface_mask, phase_labels=phase_labels, phase_diffusivity=phase_diffusivity)


def thomas(lower_band, main_band, upper_band, right_side):
    def forward(carried, row_items):
        ratio_prev, value_prev = carried
        lower_row, main_row, upper_row, right_row = row_items
        pivot_value = main_row - lower_row * ratio_prev
        ratio_next = upper_row / pivot_value
        value_next = (right_row - lower_row * value_prev) / pivot_value
        return (ratio_next, value_next), (ratio_next, value_next)
    zeros_row = jnp.zeros(right_side.shape[1:], jnp.float32)
    _, (ratios, values) = lax.scan(forward, (zeros_row, zeros_row), (lower_band, main_band, upper_band, right_side))

    def backward(next_value, row_items):
        ratio_row, value_row = row_items
        result = value_row - ratio_row * next_value
        return result, result
    _, solved = lax.scan(backward, zeros_row, (ratios, values), reverse=True)
    return solved


def line_solve(diffusion_rate, right_side):
    return thomas(-diffusion_rate, 1.0 + 2.0 * diffusion_rate, -diffusion_rate, right_side)


def second_along(values, diffusion_rate, line_axis):
    leading = jnp.moveaxis(values, line_axis, 0)
    padded = jnp.pad(leading, ((1, 1), (0, 0), (0, 0)))
    neighbours = padded[2:] + padded[:-2] - 2.0 * leading
    return diffusion_rate * jnp.moveaxis(neighbours, 0, line_axis)


def reference(species_field, reaction_source, interface_mask, phase_labels, phase_diffusivity):
    diffusion_rate = 0.5 * NU * phase_diffusivity[phase_labels]
    along_y = second_along(species_field, diffusion_rate, 0)
    along_z = second_along(species_field, diffusion_rate, 1)
    along_x = second_along(species_field, diffusion_rate, 2)
    section_one = species_field + along_x + 2.0 * along_y + 2.0 * along_z + interface_mask.astype(jnp.float32) * reaction_source
    after_x = jnp.moveaxis(line_solve(jnp.moveaxis(diffusion_rate, 2, 0), jnp.moveaxis(section_one, 2, 0)), 0, 2)
    after_y = line_solve(diffusion_rate, after_x - along_y)
    section_three = after_y - along_z
    updated_field = jnp.moveaxis(line_solve(jnp.moveaxis(diffusion_rate, 1, 0), jnp.moveaxis(section_three, 1, 0)), 0, 1)
    return updated_field
```

```python
import functools

import jax
import jax.numpy as jnp
from jax import lax
from jax.experimental import pallas as pl
from jax.experimental.pallas import tpu as pltpu
from jax.sharding import PartitionSpec as P

NU = 400
LANES = 128
MESH = pl.DeviceIdType.MESH


def recip(value):
    return pl.reciprocal(value, approx=False)


def eliminate(slack, rate):
    excess = rate + slack
    ratio = recip(1.0 + excess)
    return excess * ratio, ratio


def kernel(
    ny, nz, ly, lz, lx, phases,
    diff, u_hbm, s_hbm, m_hbm, l_hbm, out_hbm,
    u_v, s_v, m_v, l_v, g_v, cy, cz, lapz, rt, cx, r2, rz, out_v,
    zh_send, zh_recv, ye_send, ye_recv, yp_send, yp_recv, ya_send, ya_recv, ze, zp,
    ychain, zchain,
    loc_sem, out_sem, hy_s, hy_r, hz_s, hz_r, ye_s, ye_r, yp_s, yp_r, ya_s, ya_r,
    ze_s, ze_r, zp_s, zp_r,
):
    halves = lx // LANES
    rows = ly * lz
    blocks = rows // LANES
    per_block = LANES // lz
    rp = lz // ny
    half_x = lx // 2
    me_y = lax.axis_index("gy")
    me_z = lax.axis_index("gz")
    up_y, down_y = lax.rem(me_y + 1, ny), lax.rem(me_y + ny - 1, ny)
    up_z, down_z = lax.rem(me_z + 1, nz), lax.rem(me_z + nz - 1, nz)

    loads = []
    for index, (src, dst) in enumerate(((l_hbm, l_v), (u_hbm, u_v), (s_hbm, s_v), (m_hbm, m_v))):
        pair = []
        for h in range(halves):
            target = dst[h].at[pl.ds(1, ly)] if dst is u_v else dst[h]
            copy = pltpu.make_async_copy(
                src.at[:, :, pl.ds(h * LANES, LANES)], target, loc_sem.at[index, h]
            )
            copy.start()
            pair.append(copy)
        loads.append(pair)

    barrier = pltpu.get_barrier_semaphore()

    def greet(axis, me, n):
        def one(o, _):
            pl.semaphore_signal(
                barrier, inc=1, device_id={axis: lax.rem(me + o, n)}, device_id_type=MESH
            )
            return 0
        lax.fori_loop(1, n, one, 0)

    greet("gy", me_y, ny)
    greet("gz", me_z, nz)
    pl.semaphore_wait(barrier, ny + nz - 2)

    halo_y = []
    for h in range(halves):
        cols = pl.ds(h * LANES, LANES)
        for d, (row, place, peer) in enumerate(((ly - 1, 0, up_y), (0, ly + 1, down_y))):
            copy = pltpu.make_async_remote_copy(
                src_ref=u_hbm.at[row, :, cols], dst_ref=u_v[h].at[place],
                send_sem=hy_s.at[h, d], recv_sem=hy_r.at[h, d],
                device_id={"gy": peer}, device_id_type=MESH,
            )
            copy.start()
            halo_y.append(copy)

    for h in range(halves):
        loads[1][h].wait()
        for d, z in ((0, lz - 1), (1, 0)):
            def pick(y, _):
                zh_send[d, h, pl.ds(y, 1), :] = u_v[h][y + 1, pl.ds(z, 1), :]
                return 0
            lax.fori_loop(0, ly, pick, 0, unroll=8)
    halo_z = []
    for d, peer in ((0, up_z), (1, down_z)):
        copy = pltpu.make_async_remote_copy(
            src_ref=zh_send.at[d], dst_ref=zh_recv.at[d],
            send_sem=hz_s.at[d], recv_sem=hz_r.at[d],
            device_id={"gz": peer}, device_id_type=MESH,
        )
        copy.start()
        halo_z.append(copy)

    def spread(axis, me, n, source, target, send, recv, start):
        def one(o, _):
            peer = lax.rem(me + o, n)
            if start:
                pltpu.make_async_remote_copy(
                    src_ref=source(peer), dst_ref=target(me),
                    send_sem=send(peer), recv_sem=recv(me),
                    device_id={axis: peer}, device_id_type=MESH,
                ).start()
            else:
                copy = pltpu.make_async_remote_copy(
                    src_ref=source(peer), dst_ref=target(peer),
                    send_sem=send(peer), recv_sem=recv(peer),
                    device_id={axis: peer}, device_id_type=MESH,
                )
                copy.wait_send()
                copy.wait_recv()
            return 0
        lax.fori_loop(1, n, one, 0)

    def ye_do(start):
        spread("gy", me_y, ny, lambda p: ye_send.at[p], lambda p: ye_recv.at[p],
               lambda p: ye_s.at[p], lambda p: ye_r.at[p], start)

    def yp_do(h, start):
        spread("gy", me_y, ny, lambda p: yp_send.at[h, p], lambda p: yp_recv.at[h, p],
               lambda p: yp_s.at[h, p], lambda p: yp_r.at[h, p], start)

    def ya_do(h, start):
        spread("gy", me_y, ny, lambda p: ya_send.at[h, p], lambda p: ya_recv.at[h, p],
               lambda p: ya_s.at[h, p], lambda p: ya_r.at[h, p], start)

    def ze_do(start):
        spread("gz", me_z, nz, lambda p: ze.at[me_z], lambda p: ze.at[p],
               lambda p: ze_s.at[p], lambda p: ze_r.at[p], start)

    def zp_do(h, start):
        spread("gz", me_z, nz, lambda p: zp.at[h, me_z], lambda p: zp.at[h, p],
               lambda p: zp_s.at[h, p], lambda p: zp_r.at[h, p], start)

    inv = [recip(0.5 * NU * jnp.full((8, LANES), diff[k], jnp.float32))[:1] for k in range(phases)]
    plane = (lz, LANES)
    ones, zeros = jnp.ones(plane, jnp.float32), jnp.zeros(plane, jnp.float32)
    for h in range(halves):
        loads[0][h].wait()

        def matrix_y(y, carry):
            slack, prod, low, _ = carry
            at = pl.ds(pl.multiple_of(y * lz, lz), lz)
            label = l_v[h][y]
            rate = jnp.broadcast_to(inv[0], plane)
            for k in range(1, phases):
                rate = jnp.where(label == k, inv[k], rate)
            g_v[h][at, :] = rate
            slack, ratio = eliminate(slack, rate)
            cy[h][at, :] = ratio
            later = prod * ratio
            return slack, later, low + prod * later, ratio

        _, prod, low, last = lax.fori_loop(0, ly, matrix_y, (ones, ones, zeros, zeros))
        for j in range(ny):
            part = slice(rp * j, rp * (j + 1))
            ye_send[j, h, 0] = low[part]
            ye_send[j, h, 1] = prod[part]
            ye_send[j, h, 2] = last[part]
    ye_recv[me_y] = ye_send[me_y]
    ye_do(True)

    slab = (ly, LANES)
    zones, zzeros = jnp.ones(slab, jnp.float32), jnp.zeros(slab, jnp.float32)
    for h in range(halves):
        def matrix_z(z, carry):
            slack, prod, low, _ = carry
            rate = g_v[h][pl.ds(z, ly, stride=lz), :]
            slack, ratio = eliminate(slack, rate)
            cz[h][z] = ratio
            later = prod * ratio
            return slack, later, low + prod * later, ratio

        _, prod, low, last = lax.fori_loop(
            0, lz, matrix_z, (zones, zzeros + 1.0, zzeros, zzeros), unroll=2
        )
        ze[me_z, h, 0] = low
        ze[me_z, h, 1] = prod
        ze[me_z, h, 2] = last
    ze_do(True)

    for h in range(halves):
        def turn_g(b, _):
            block = g_v[h][pl.ds(pl.multiple_of(b * LANES, LANES), LANES), :]
            cx[pl.ds(h * LANES * blocks + b, LANES, stride=blocks), :] = block.T
            return 0
        lax.fori_loop(0, blocks, turn_g, 0, unroll=2)

    def at_x(i):
        return pl.ds(pl.multiple_of(i * blocks, blocks), blocks)

    lines = (blocks, LANES)
    lone, lzero = jnp.ones(lines, jnp.float32), jnp.zeros(lines, jnp.float32)

    def matrix_x(i, carry):
        one, two = carry
        one, ratio = eliminate(one, cx[at_x(i), :])
        cx[at_x(i), :] = ratio
        two, ratio = eliminate(two, cx[at_x(lx - 1 - i), :])
        cx[at_x(lx - 1 - i), :] = ratio
        return one, two

    slack_one, slack_two = lax.fori_loop(0, half_x, matrix_x, (lone, lone), unroll=4)
    middle = recip(slack_one + slack_two - slack_one * slack_two)

    for copy in halo_y + halo_z:
        copy.wait()
    for h in range(halves):
        loads[2][h].wait()
        loads[3][h].wait()

        @pl.when(me_y == 0)
        def _():
            u_v[h][0] = zeros

        @pl.when(me_y == ny - 1)
        def _():
            u_v[h][ly + 1] = zeros

        @pl.when(me_z == 0)
        def _():
            zh_recv[0, h] = zzeros

        @pl.when(me_z == nz - 1)
        def _():
            zh_recv[1, h] = zzeros

    sub = lax.broadcasted_iota(jnp.int32, plane, 0)
    lane = lax.broadcasted_iota(jnp.int32, plane, 1)

    def right_x(b, _):
        done = [[] for _ in range(halves)]
        for k in range(per_block):
            y = b * per_block + k
            at = pl.ds(pl.multiple_of(y * lz, lz), lz)
            mids = [u_v[h][y + 1] for h in range(halves)]
            ups = [pltpu.roll(m, LANES - 1, 1) for m in mids]
            downs = [pltpu.roll(m, 1, 1) for m in mids]
            for h in range(halves):
                mid = mids[h]
                after = jnp.where(lane == LANES - 1, ups[h + 1] if h + 1 < halves else 0.0, ups[h])
                before = jnp.where(lane == 0, downs[h - 1] if h else 0.0, downs[h])
                twice = 2.0 * mid
                lap_x = after + before - twice
                lap_y = u_v[h][y] + u_v[h][y + 2] - twice
                below = jnp.where(sub == 0, zh_recv[0, h, pl.ds(y, 1), :], pltpu.roll(mid, 1, 0))
                above = jnp.where(
                    sub == lz - 1, zh_recv[1, h, pl.ds(y, 1), :], pltpu.roll(mid, lz - 1, 0)
                )
                lap_z = below + above - twice
                lapz[h][at, :] = lap_z
                source = m_v[h][y].astype(jnp.float32) * s_v[h][y]
                value = g_v[h][at, :] * (mid + source) + (lap_x + 2.0 * (lap_y + lap_z))
                done[h].append(value)
        for h in range(halves):
            block = jnp.concatenate(done[h], 0)
            rt[pl.ds(h * LANES * blocks + b, LANES, stride=blocks), :] = block.T
        return 0

    lax.fori_loop(0, blocks, right_x, 0)

    def forward_x(i, carry):
        one, two = carry
        low_at, high_at = at_x(i), at_x(lx - 1 - i)
        one = (rt[low_at, :] + one) * cx[low_at, :]
        rt[low_at, :] = one
        two = (rt[high_at, :] + two) * cx[high_at, :]
        rt[high_at, :] = two
        return one, two

    one, two = lax.fori_loop(0, half_x, forward_x, (lzero, lzero), unroll=8)
    low_mid, high_mid = at_x(half_x - 1), at_x(half_x)
    first = (one + cx[low_mid, :] * two) * middle
    second = (two + cx[high_mid, :] * one) * middle
    rt[low_mid, :] = first
    rt[high_mid, :] = second

    def backward_x(i, carry):
        one, two = carry
        low_at, high_at = at_x(half_x - 1 - i), at_x(half_x + i)
        one = rt[low_at, :] + cx[low_at, :] * one
        rt[low_at, :] = one
        two = rt[high_at, :] + cx[high_at, :] * two
        rt[high_at, :] = two
        return one, two

    lax.fori_loop(1, half_x, backward_x, (first, second), unroll=8)

    for h in range(halves):
        def local_y(b, carry):
            value, prod, head = carry
            block = rt[pl.ds(h * LANES * blocks + b, LANES, stride=blocks), :].T
            for k in range(per_block):
                y = b * per_block + k
                at = pl.ds(pl.multiple_of(y * lz, lz), lz)
                lap_y = u_v[h][y] + u_v[h][y + 2] - 2.0 * u_v[h][y + 1]
                right = g_v[h][at, :] * block[k * lz:(k + 1) * lz] - lap_y
                r2[h][at, :] = right
                ratio = cy[h][at, :]
                value = (right + value) * ratio
                head = head + value * prod
                prod = prod * ratio
            return value, prod, head

        value, _, head = lax.fori_loop(0, blocks, local_y, (zeros, ones, zeros))
        for j in range(ny):
            part = slice(rp * j, rp * (j + 1))
            yp_send[h, j, 0] = head[part]
            yp_send[h, j, 1] = value[part]
        yp_recv[h, me_y] = yp_send[h, me_y]
        yp_do(h, True)

    def chain(n, coef, plain, keep, answer, shape):
        none = jnp.zeros(shape, jnp.float32)

        def forward(k, carry):
            offset, slope = carry
            low, cross, high = coef(k, 0), coef(k, 1), coef(k, 2)
            pivot = recip(1.0 - low * slope)
            head = pivot * (plain(k, 0) + low * offset)
            keep[k, 0] = offset
            keep[k, 1] = slope
            keep[k, 2] = head
            keep[k, 3] = pivot * cross
            return (
                plain(k, 1) + cross * (offset + slope * head),
                high + cross * cross * slope * pivot,
            )

        lax.fori_loop(0, n, forward, (none, none))

        def backward(i, after):
            k = n - 1 - i
            head = keep[k, 2] + keep[k, 3] * after
            answer(k, keep[k, 0] + keep[k, 1] * head, after)
            return head

        lax.fori_loop(0, n, backward, none)

    ye_do(False)
    for h in range(halves):
        yp_do(h, False)

        def answer_y(k, left, right):
            ya_send[h, k, 0] = left
            ya_send[h, k, 1] = right

        chain(ny, lambda k, c: ye_recv[k, h, c], lambda k, c: yp_recv[h, k, c],
              ychain, answer_y, (rp, LANES))
        ya_recv[h, me_y] = ya_send[h, me_y]
        ya_do(h, True)

    for h in range(halves):
        ya_do(h, False)
        left = jnp.concatenate([ya_recv[h, j, 0] for j in range(ny)], 0)
        right = jnp.concatenate([ya_recv[h, j, 1] for j in range(ny)], 0)

        def forward_y(y, value):
            at = pl.ds(pl.multiple_of(y * lz, lz), lz)
            value = (r2[h][at, :] + value) * cy[h][at, :]
            r2[h][at, :] = value
            return value

        lax.fori_loop(0, ly, forward_y, left, unroll=2)

        def backward_y(i, value):
            y = ly - 1 - i
            at = pl.ds(pl.multiple_of(y * lz, lz), lz)
            value = r2[h][at, :] + cy[h][at, :] * value
            rz[h][pl.ds(y, lz, stride=ly), :] = g_v[h][at, :] * value - lapz[h][at, :]
            return value

        lax.fori_loop(0, ly, backward_y, right, unroll=2)

        def local_z(z, carry):
            value, prod, head = carry
            ratio = cz[h][z]
            value = (rz[h][pl.ds(pl.multiple_of(z * ly, ly), ly), :] + value) * ratio
            return value, prod * ratio, head + value * prod

        value, _, head = lax.fori_loop(0, lz, local_z, (zzeros, zones, zzeros), unroll=4)
        zp[h, me_z, 0] = head
        zp[h, me_z, 1] = value
        zp_do(h, True)

    ze_do(False)
    for h in range(halves):
        zp_do(h, False)

        def answer_z(k, left, right):
            zchain[k, 4] = left
            zchain[k, 5] = right

        chain(nz, lambda k, c: ze[k, h, c], lambda k, c: zp[h, k, c], zchain, answer_z, slab)
        left, right = zchain[me_z, 4], zchain[me_z, 5]

        def forward_z(z, value):
            at = pl.ds(pl.multiple_of(z * ly, ly), ly)
            value = (rz[h][at, :] + value) * cz[h][z]
            rz[h][at, :] = value
            return value

        lax.fori_loop(0, lz, forward_z, left, unroll=4)

        def backward_z(i, value):
            z = lz - 1 - i
            value = rz[h][pl.ds(pl.multiple_of(z * ly, ly), ly), :] + cz[h][z] * value
            out_v[h][pl.ds(z, ly, stride=lz), :] = value
            return value

        lax.fori_loop(0, lz, backward_z, right, unroll=4)

        def send_out(y, _):
            pltpu.make_async_copy(
                out_v[h].at[pl.ds(pl.multiple_of(y * lz, lz), lz), :],
                out_hbm.at[y, :, pl.ds(h * LANES, LANES)], out_sem.at[h, y],
            ).start()
            return 0

        lax.fori_loop(0, ly, send_out, 0)

    for h in range(halves):
        def wait_out(y, _):
            pltpu.make_async_copy(
                out_v[h].at[pl.ds(pl.multiple_of(y * lz, lz), lz), :],
                out_hbm.at[y, :, pl.ds(h * LANES, LANES)], out_sem.at[h, y],
            ).wait()
            return 0

        lax.fori_loop(0, ly, wait_out, 0)


def body(ny, nz, species_field, reaction_source, interface_mask, phase_labels, phase_diffusivity):
    ly, lz, lx = species_field.shape
    halves = lx // LANES
    rows = ly * lz
    blocks = rows // LANES
    rp = lz // ny
    f32 = jnp.float32

    def vm(*shape, dtype=f32):
        return pltpu.VMEM(shape, dtype)

    def pair(*shape, dtype=f32):
        return [vm(*shape, dtype=dtype) for _ in range(halves)]

    def sems(*shape):
        return pltpu.SemaphoreType.DMA(shape)

    scratch = [
        pair(ly + 2, lz, LANES), pair(ly, lz, LANES),
        pair(ly, lz, LANES, dtype=jnp.int32), pair(ly, lz, LANES, dtype=jnp.int32),
        pair(rows, LANES), pair(rows, LANES), pair(lz, ly, LANES), pair(rows, LANES),
        vm(lx * blocks, LANES), vm(lx * blocks, LANES),
        pair(rows, LANES), pair(rows, LANES), pair(rows, LANES),
        vm(2, halves, ly, LANES), vm(2, halves, ly, LANES),
        vm(ny, halves, 3, rp, LANES), vm(ny, halves, 3, rp, LANES),
        vm(halves, ny, 2, rp, LANES), vm(halves, ny, 2, rp, LANES),
        vm(halves, ny, 2, rp, LANES), vm(halves, ny, 2, rp, LANES),
        vm(nz, halves, 3, ly, LANES), vm(halves, nz, 2, ly, LANES),
        vm(ny, 4, rp, LANES), vm(nz, 6, ly, LANES),
        sems(4, halves), sems(halves, ly),
        sems(halves, 2), sems(halves, 2), sems(2), sems(2),
        sems(ny), sems(ny), sems(halves, ny), sems(halves, ny), sems(halves, ny), sems(halves, ny),
        sems(nz), sems(nz), sems(halves, nz), sems(halves, nz),
    ]
    anywhere = pl.BlockSpec(memory_space=pl.ANY)
    return pl.pallas_call(
        functools.partial(kernel, ny, nz, ly, lz, lx, phase_diffusivity.shape[0]),
        out_shape=jax.ShapeDtypeStruct(species_field.shape, f32),
        in_specs=[pl.BlockSpec(memory_space=pltpu.SMEM)] + [anywhere] * 4,
        out_specs=anywhere,
        scratch_shapes=scratch,
        compiler_params=pltpu.CompilerParams(
            collective_id=0, has_side_effects=True, vmem_limit_bytes=56 * 1024 * 1024
        ),
    )(phase_diffusivity, species_field, reaction_source, interface_mask, phase_labels)


def solution(mesh):
    spec = P("gy", "gz", None)
    return jax.shard_map(
        functools.partial(body, mesh.shape["gy"], mesh.shape["gz"]),
        mesh=mesh, in_specs=(spec,) * 4 + (P(),), out_specs=spec, check_vma=False,
    )
```

```python
import functools

import jax
import jax.numpy as jnp
from jax import lax
from jax.experimental import pallas as pl
from jax.experimental.pallas import tpu as pltpu
from jax.sharding import PartitionSpec as P

NU = 400
LANES = 128
MESH = pl.DeviceIdType.MESH


def recip(value):
    return pl.reciprocal(value, approx=False)


def eliminate(slack, rate):
    excess = rate + slack
    ratio = recip(1.0 + excess)
    return excess * ratio, ratio


def kernel(
    ny, nz, ly, lz, lx, phases,
    diff, u_hbm, s_hbm, m_hbm, l_hbm, out,
    u_v, s_v, m_v, l_v, g_v, cy, cz, lapz, rt, cx, r2, rz,
    zh_send, zh_recv, ye_send, ye_recv, yp_send, yp_recv, ya_send, ya_recv, ze, zp,
    ychain, zchain,
    loc_sem, hy_s, hy_r, hz_s, hz_r, ye_s, ye_r, yp_s, yp_r, ya_s, ya_r,
    ze_s, ze_r, zp_s, zp_r,
):
    halves = lx // LANES
    rows = ly * lz
    blocks = rows // LANES
    per_block = LANES // lz
    rp = lz // ny
    half_x = lx // 2
    pitch_x, pitch_z = blocks + 1, ly + 1
    me_y = lax.axis_index("gy")
    me_z = lax.axis_index("gz")
    up_y, down_y = lax.rem(me_y + 1, ny), lax.rem(me_y + ny - 1, ny)
    up_z, down_z = lax.rem(me_z + 1, nz), lax.rem(me_z + nz - 1, nz)

    loads = []
    for index, (src, dst) in enumerate(((l_hbm, l_v), (u_hbm, u_v), (s_hbm, s_v), (m_hbm, m_v))):
        pair = []
        for h in range(halves):
            target = dst[h].at[pl.ds(1, ly)] if dst is u_v else dst[h]
            copy = pltpu.make_async_copy(
                src.at[:, :, pl.ds(h * LANES, LANES)], target, loc_sem.at[index, h]
            )
            copy.start()
            pair.append(copy)
        loads.append(pair)

    barrier = pltpu.get_barrier_semaphore()

    def greet(axis, me, n):
        def one(o, _):
            pl.semaphore_signal(
                barrier, inc=1, device_id={axis: lax.rem(me + o, n)}, device_id_type=MESH
            )
            return 0
        lax.fori_loop(1, n, one, 0)

    greet("gy", me_y, ny)
    greet("gz", me_z, nz)
    pl.semaphore_wait(barrier, ny + nz - 2)

    halo_y = []
    for h in range(halves):
        cols = pl.ds(h * LANES, LANES)
        for d, (row, place, peer) in enumerate(((ly - 1, 0, up_y), (0, ly + 1, down_y))):
            copy = pltpu.make_async_remote_copy(
                src_ref=u_hbm.at[row, :, cols], dst_ref=u_v[h].at[place],
                send_sem=hy_s.at[h, d], recv_sem=hy_r.at[h, d],
                device_id={"gy": peer}, device_id_type=MESH,
            )
            copy.start()
            halo_y.append(copy)

    for h in range(halves):
        loads[1][h].wait()
        for d, z in ((0, lz - 1), (1, 0)):
            def pick(y, _):
                zh_send[d, h, pl.ds(y, 1), :] = u_v[h][y + 1, pl.ds(z, 1), :]
                return 0
            lax.fori_loop(0, ly, pick, 0, unroll=8)
    halo_z = []
    for d, peer in ((0, up_z), (1, down_z)):
        copy = pltpu.make_async_remote_copy(
            src_ref=zh_send.at[d], dst_ref=zh_recv.at[d],
            send_sem=hz_s.at[d], recv_sem=hz_r.at[d],
            device_id={"gz": peer}, device_id_type=MESH,
        )
        copy.start()
        halo_z.append(copy)

    def spread(axis, me, n, source, target, send, recv, start):
        def one(o, _):
            peer = lax.rem(me + o, n)
            if start:
                pltpu.make_async_remote_copy(
                    src_ref=source(peer), dst_ref=target(me),
                    send_sem=send(peer), recv_sem=recv(me),
                    device_id={axis: peer}, device_id_type=MESH,
                ).start()
            else:
                copy = pltpu.make_async_remote_copy(
                    src_ref=source(peer), dst_ref=target(peer),
                    send_sem=send(peer), recv_sem=recv(peer),
                    device_id={axis: peer}, device_id_type=MESH,
                )
                copy.wait_send()
                copy.wait_recv()
            return 0
        lax.fori_loop(1, n, one, 0)

    def ye_do(start):
        spread("gy", me_y, ny, lambda p: ye_send.at[p], lambda p: ye_recv.at[p],
               lambda p: ye_s.at[p], lambda p: ye_r.at[p], start)

    def yp_do(h, start):
        spread("gy", me_y, ny, lambda p: yp_send.at[h, p], lambda p: yp_recv.at[h, p],
               lambda p: yp_s.at[h, p], lambda p: yp_r.at[h, p], start)

    def ya_do(h, start):
        spread("gy", me_y, ny, lambda p: ya_send.at[h, p], lambda p: ya_recv.at[h, p],
               lambda p: ya_s.at[h, p], lambda p: ya_r.at[h, p], start)

    def ze_do(start):
        spread("gz", me_z, nz, lambda p: ze.at[me_z], lambda p: ze.at[p],
               lambda p: ze_s.at[p], lambda p: ze_r.at[p], start)

    def zp_do(h, start):
        spread("gz", me_z, nz, lambda p: zp.at[h, me_z], lambda p: zp.at[h, p],
               lambda p: zp_s.at[h, p], lambda p: zp_r.at[h, p], start)

    inv = [recip(0.5 * NU * jnp.full((8, LANES), diff[k], jnp.float32))[:1] for k in range(phases)]
    slab = (ly, LANES)
    zones, zzeros = jnp.ones(slab, jnp.float32), jnp.zeros(slab, jnp.float32)
    plane = (lz, LANES)
    ones, zeros = jnp.ones(plane, jnp.float32), jnp.zeros(plane, jnp.float32)
    for h in range(halves):
        loads[0][h].wait()

        def matrix_y(y, carry):
            slack, prod, low, _ = carry
            at = pl.ds(pl.multiple_of(y * lz, lz), lz)
            label = l_v[h][y]
            rate = jnp.broadcast_to(inv[0], plane)
            for k in range(1, phases):
                rate = jnp.where(label == k, inv[k], rate)
            g_v[h][at, :] = rate
            rz[h][pl.ds(y, lz, stride=pitch_z), :] = rate
            slack, ratio = eliminate(slack, rate)
            cy[h][at, :] = ratio
            later = prod * ratio
            return slack, later, low + prod * later, ratio

        _, prod, low, last = lax.fori_loop(0, ly, matrix_y, (ones, ones, zeros, zeros))
        for j in range(ny):
            part = slice(rp * j, rp * (j + 1))
            ye_send[j, h, 0] = low[part]
            ye_send[j, h, 1] = prod[part]
            ye_send[j, h, 2] = last[part]
    ye_recv[me_y] = ye_send[me_y]
    ye_do(True)

    for h in range(halves):
        def turn_g(b, _):
            block = g_v[h][pl.ds(pl.multiple_of(b * LANES, LANES), LANES), :]
            cx[pl.ds(h * LANES * pitch_x + b, LANES, stride=pitch_x), :] = block.T
            return 0
        lax.fori_loop(0, blocks, turn_g, 0, unroll=2)

    def at_x(i):
        return pl.ds(i * pitch_x, blocks)

    lines = (blocks, LANES)
    lone, lzero = jnp.ones(lines, jnp.float32), jnp.zeros(lines, jnp.float32)

    def matrix_x(i, carry):
        one, two = carry
        one, ratio = eliminate(one, cx[at_x(i), :])
        cx[at_x(i), :] = ratio
        two, ratio = eliminate(two, cx[at_x(lx - 1 - i), :])
        cx[at_x(lx - 1 - i), :] = ratio
        return one, two

    slack_one, slack_two = lax.fori_loop(0, half_x, matrix_x, (lone, lone), unroll=4)
    middle = recip(slack_one + slack_two - slack_one * slack_two)

    for copy in halo_y + halo_z:
        copy.wait()
    for h in range(halves):
        loads[2][h].wait()
        loads[3][h].wait()

        @pl.when(me_y == 0)
        def _():
            u_v[h][0] = zeros

        @pl.when(me_y == ny - 1)
        def _():
            u_v[h][ly + 1] = zeros

        @pl.when(me_z == 0)
        def _():
            zh_recv[0, h] = zzeros

        @pl.when(me_z == nz - 1)
        def _():
            zh_recv[1, h] = zzeros

    sub = lax.broadcasted_iota(jnp.int32, plane, 0)
    lane = lax.broadcasted_iota(jnp.int32, plane, 1)

    def right_x(b, _):
        done = [[] for _ in range(halves)]
        for k in range(per_block):
            y = b * per_block + k
            at = pl.ds(pl.multiple_of(y * lz, lz), lz)
            mids = [u_v[h][y + 1] for h in range(halves)]
            ups = [pltpu.roll(m, LANES - 1, 1) for m in mids]
            downs = [pltpu.roll(m, 1, 1) for m in mids]
            for h in range(halves):
                mid = mids[h]
                after = jnp.where(lane == LANES - 1, ups[h + 1] if h + 1 < halves else 0.0, ups[h])
                before = jnp.where(lane == 0, downs[h - 1] if h else 0.0, downs[h])
                twice = 2.0 * mid
                lap_x = after + before - twice
                lap_y = u_v[h][y] + u_v[h][y + 2] - twice
                below = jnp.where(sub == 0, zh_recv[0, h, pl.ds(y, 1), :], pltpu.roll(mid, 1, 0))
                above = jnp.where(
                    sub == lz - 1, zh_recv[1, h, pl.ds(y, 1), :], pltpu.roll(mid, lz - 1, 0)
                )
                lap_z = below + above - twice
                lapz[h][at, :] = lap_z
                source = m_v[h][y].astype(jnp.float32) * s_v[h][y]
                value = g_v[h][at, :] * (mid + source) + (lap_x + 2.0 * (lap_y + lap_z))
                done[h].append(value)
        for h in range(halves):
            block = jnp.concatenate(done[h], 0)
            rt[pl.ds(h * LANES * pitch_x + b, LANES, stride=pitch_x), :] = block.T
        return 0

    lax.fori_loop(0, blocks, right_x, 0)

    def forward_x(i, carry):
        one, two = carry
        low_at, high_at = at_x(i), at_x(lx - 1 - i)
        one = (rt[low_at, :] + one) * cx[low_at, :]
        rt[low_at, :] = one
        two = (rt[high_at, :] + two) * cx[high_at, :]
        rt[high_at, :] = two
        return one, two

    one, two = lax.fori_loop(0, half_x, forward_x, (lzero, lzero), unroll=8)
    low_mid, high_mid = at_x(half_x - 1), at_x(half_x)
    first = (one + cx[low_mid, :] * two) * middle
    second = (two + cx[high_mid, :] * one) * middle
    rt[low_mid, :] = first
    rt[high_mid, :] = second

    def backward_x(i, carry):
        one, two = carry
        low_at, high_at = at_x(half_x - 1 - i), at_x(half_x + i)
        one = rt[low_at, :] + cx[low_at, :] * one
        rt[low_at, :] = one
        two = rt[high_at, :] + cx[high_at, :] * two
        rt[high_at, :] = two
        return one, two

    lax.fori_loop(1, half_x, backward_x, (first, second), unroll=8)

    for h in range(halves):
        def local_y(b, carry):
            value, prod, head = carry
            block = rt[pl.ds(h * LANES * pitch_x + b, LANES, stride=pitch_x), :].T
            for k in range(per_block):
                y = b * per_block + k
                at = pl.ds(pl.multiple_of(y * lz, lz), lz)
                lap_y = u_v[h][y] + u_v[h][y + 2] - 2.0 * u_v[h][y + 1]
                right = g_v[h][at, :] * block[k * lz:(k + 1) * lz] - lap_y
                r2[h][at, :] = right
                ratio = cy[h][at, :]
                value = (right + value) * ratio
                head = head + value * prod
                prod = prod * ratio
            return value, prod, head

        value, _, head = lax.fori_loop(0, blocks, local_y, (zeros, ones, zeros))
        for j in range(ny):
            part = slice(rp * j, rp * (j + 1))
            yp_send[h, j, 0] = head[part]
            yp_send[h, j, 1] = value[part]
        yp_recv[h, me_y] = yp_send[h, me_y]
        yp_do(h, True)

    def pivots(n, coef, keep, shape):
        def one(k, slope):
            low, cross = coef(k, 0), coef(k, 1)
            pivot = recip(1.0 - low * slope)
            keep[k, 0] = slope
            keep[k, 1] = pivot
            keep[k, 2] = pivot * cross
            return coef(k, 2) + cross * cross * slope * pivot

        lax.fori_loop(0, n, one, jnp.zeros(shape, jnp.float32))

    def chain(n, coef, plain, keep, answer, shape):
        none = jnp.zeros(shape, jnp.float32)

        def forward(k, offset):
            head = keep[k, 1] * (plain(k, 0) + coef(k, 0) * offset)
            keep[k, 3] = offset
            keep[k, 4] = head
            return plain(k, 1) + coef(k, 1) * (offset + keep[k, 0] * head)

        lax.fori_loop(0, n, forward, none)

        def backward(i, after):
            k = n - 1 - i
            head = keep[k, 4] + keep[k, 2] * after
            answer(k, keep[k, 3] + keep[k, 0] * head, after)
            return head

        lax.fori_loop(0, n, backward, none)

    for h in range(halves):
        def matrix_z(z, carry):
            slack, prod, low, _ = carry
            rate = rz[h][pl.ds(z * pitch_z, ly), :]
            slack, ratio = eliminate(slack, rate)
            cz[h][z] = ratio
            later = prod * ratio
            return slack, later, low + prod * later, ratio

        _, prod, low, last = lax.fori_loop(
            0, lz, matrix_z, (zones, zzeros + 1.0, zzeros, zzeros), unroll=2
        )
        ze[me_z, h, 0] = low
        ze[me_z, h, 1] = prod
        ze[me_z, h, 2] = last
    ze_do(True)

    ye_do(False)
    for h in range(halves):
        pivots(ny, lambda k, c: ye_recv[k, h, c], ychain.at[h], (rp, LANES))
    for h in range(halves):
        yp_do(h, False)

        def answer_y(k, left, right):
            ya_send[h, k, 0] = left
            ya_send[h, k, 1] = right

        chain(ny, lambda k, c: ye_recv[k, h, c], lambda k, c: yp_recv[h, k, c],
              ychain.at[h], answer_y, (rp, LANES))
        ya_recv[h, me_y] = ya_send[h, me_y]
        ya_do(h, True)

    ze_do(False)
    for h in range(halves):
        pivots(nz, lambda k, c: ze[k, h, c], zchain.at[h], slab)

    for h in range(halves):
        ya_do(h, False)
        left = jnp.concatenate([ya_recv[h, j, 0] for j in range(ny)], 0)
        right = jnp.concatenate([ya_recv[h, j, 1] for j in range(ny)], 0)

        def forward_y(y, value):
            at = pl.ds(pl.multiple_of(y * lz, lz), lz)
            value = (r2[h][at, :] + value) * cy[h][at, :]
            r2[h][at, :] = value
            return value

        lax.fori_loop(0, ly, forward_y, left, unroll=2)

        def backward_y(i, value):
            y = ly - 1 - i
            at = pl.ds(pl.multiple_of(y * lz, lz), lz)
            value = r2[h][at, :] + cy[h][at, :] * value
            rz[h][pl.ds(y, lz, stride=pitch_z), :] = g_v[h][at, :] * value - lapz[h][at, :]
            return value

        lax.fori_loop(0, ly, backward_y, right, unroll=2)

        def local_z(z, carry):
            value, prod, head = carry
            ratio = cz[h][z]
            value = (rz[h][pl.ds(z * pitch_z, ly), :] + value) * ratio
            return value, prod * ratio, head + value * prod

        value, _, head = lax.fori_loop(0, lz, local_z, (zzeros, zones, zzeros), unroll=4)
        zp[h, me_z, 0] = head
        zp[h, me_z, 1] = value
        zp_do(h, True)

    for h in range(halves):
        zp_do(h, False)

        def answer_z(k, left, right):
            zchain[h, k, 5] = left
            zchain[h, k, 6] = right

        chain(nz, lambda k, c: ze[k, h, c], lambda k, c: zp[h, k, c],
              zchain.at[h], answer_z, slab)
        left, right = zchain[h, me_z, 5], zchain[h, me_z, 6]

        def forward_z(z, value):
            at = pl.ds(z * pitch_z, ly)
            value = (rz[h][at, :] + value) * cz[h][z]
            rz[h][at, :] = value
            return value

        lax.fori_loop(0, lz, forward_z, left, unroll=4)

        def backward_z(i, value):
            z = lz - 1 - i
            value = rz[h][pl.ds(z * pitch_z, ly), :] + cz[h][z] * value
            rz[h][pl.ds(z * pitch_z, ly), :] = value
            return value

        lax.fori_loop(0, lz, backward_z, right, unroll=4)

        def turn_out(y, _):
            out[y, :, pl.ds(h * LANES, LANES)] = rz[h][pl.ds(y, lz, stride=pitch_z), :]
            return 0

        lax.fori_loop(0, ly, turn_out, 0, unroll=4)


def body(ny, nz, species_field, reaction_source, interface_mask, phase_labels, phase_diffusivity):
    ly, lz, lx = species_field.shape
    halves = lx // LANES
    rows = ly * lz
    blocks = rows // LANES
    rp = lz // ny
    f32 = jnp.float32

    def vm(*shape, dtype=f32):
        return pltpu.VMEM(shape, dtype)

    def pair(*shape, dtype=f32):
        return [vm(*shape, dtype=dtype) for _ in range(halves)]

    def sems(*shape):
        return pltpu.SemaphoreType.DMA(shape)

    scratch = [
        pair(ly + 2, lz, LANES), pair(ly, lz, LANES),
        pair(ly, lz, LANES, dtype=jnp.int32), pair(ly, lz, LANES, dtype=jnp.int32),
        pair(rows, LANES), pair(rows, LANES), pair(lz, ly, LANES), pair(rows, LANES),
        vm(lx * (blocks + 1), LANES), vm(lx * (blocks + 1), LANES),
        pair(rows, LANES), pair(lz * (ly + 1), LANES),
        vm(2, halves, ly, LANES), vm(2, halves, ly, LANES),
        vm(ny, halves, 3, rp, LANES), vm(ny, halves, 3, rp, LANES),
        vm(halves, ny, 2, rp, LANES), vm(halves, ny, 2, rp, LANES),
        vm(halves, ny, 2, rp, LANES), vm(halves, ny, 2, rp, LANES),
        vm(nz, halves, 3, ly, LANES), vm(halves, nz, 2, ly, LANES),
        vm(halves, ny, 5, rp, LANES), vm(halves, nz, 7, ly, LANES),
        sems(4, halves),
        sems(halves, 2), sems(halves, 2), sems(2), sems(2),
        sems(ny), sems(ny), sems(halves, ny), sems(halves, ny), sems(halves, ny), sems(halves, ny),
        sems(nz), sems(nz), sems(halves, nz), sems(halves, nz),
    ]
    anywhere = pl.BlockSpec(memory_space=pl.ANY)
    return pl.pallas_call(
        functools.partial(kernel, ny, nz, ly, lz, lx, phase_diffusivity.shape[0]),
        out_shape=pltpu.VMEM(species_field.shape, f32),
        in_specs=[pl.BlockSpec(memory_space=pltpu.SMEM)] + [anywhere] * 4,
        out_specs=pl.BlockSpec(memory_space=pltpu.VMEM),
        scratch_shapes=scratch,
        compiler_params=pltpu.CompilerParams(
            collective_id=0, has_side_effects=True, vmem_limit_bytes=56 * 1024 * 1024
        ),
    )(phase_diffusivity, species_field, reaction_source, interface_mask, phase_labels)


def solution(mesh):
    spec = P("gy", "gz", None)
    return jax.shard_map(
        functools.partial(body, mesh.shape["gy"], mesh.shape["gz"]),
        mesh=mesh, in_specs=(spec,) * 4 + (P(),), out_specs=spec, check_vma=False,
    )
```

```python
import functools

import jax
import jax.numpy as jnp
from jax import lax
from jax.experimental import pallas as pl
from jax.experimental.pallas import tpu as pltpu
from jax.sharding import PartitionSpec as P

NU = 400
LANES = 128
MESH = pl.DeviceIdType.MESH


def recip(value):
    return pl.reciprocal(value, approx=False)


def eliminate(slack, rate):
    excess = rate + slack
    ratio = recip(1.0 + excess)
    return excess * ratio, ratio


def kernel(
    ny, nz, ly, lz, lx, phases,
    diff, u_hbm, s_hbm, m_hbm, l_hbm, out,
    u_v, s_v, m_v, l_v, g_v, cy, cz, lapz, rt, cx, r2, rz,
    zh_send, zh_recv, ye_send, ye_recv, yp_send, yp_recv, ya_send, ya_recv, ze, zp,
    ychain, zchain,
    loc_sem, hy_s, hy_r, hz_s, hz_r, ye_s, ye_r, yp_s, yp_r, ya_s, ya_r,
    ze_s, ze_r, zp_s, zp_r,
):
    halves = lx // LANES
    rows = ly * lz
    blocks = rows // LANES
    per_block = LANES // lz
    rp = lz // ny
    half_x = lx // 2
    pitch_x, pitch_z = blocks + 1, ly + 1
    me_y = lax.axis_index("gy")
    me_z = lax.axis_index("gz")
    up_y, down_y = lax.rem(me_y + 1, ny), lax.rem(me_y + ny - 1, ny)
    up_z, down_z = lax.rem(me_z + 1, nz), lax.rem(me_z + nz - 1, nz)

    loads = []
    for index, (src, dst) in enumerate(((l_hbm, l_v), (u_hbm, u_v), (s_hbm, s_v), (m_hbm, m_v))):
        pair = []
        for h in range(halves):
            target = dst[h].at[pl.ds(1, ly)] if dst is u_v else dst[h]
            copy = pltpu.make_async_copy(
                src.at[:, :, pl.ds(h * LANES, LANES)], target, loc_sem.at[index, h]
            )
            copy.start()
            pair.append(copy)
        loads.append(pair)

    barrier = pltpu.get_barrier_semaphore()

    def greet(axis, me, n):
        def one(o, _):
            pl.semaphore_signal(
                barrier, inc=1, device_id={axis: lax.rem(me + o, n)}, device_id_type=MESH
            )
            return 0
        lax.fori_loop(1, n, one, 0)

    greet("gy", me_y, ny)
    greet("gz", me_z, nz)
    def spread(axis, me, n, source, target, send, recv, start):
        def one(o, _):
            peer = lax.rem(me + o, n)
            if start:
                pltpu.make_async_remote_copy(
                    src_ref=source(peer), dst_ref=target(me),
                    send_sem=send(peer), recv_sem=recv(me),
                    device_id={axis: peer}, device_id_type=MESH,
                ).start()
            else:
                copy = pltpu.make_async_remote_copy(
                    src_ref=source(peer), dst_ref=target(peer),
                    send_sem=send(peer), recv_sem=recv(peer),
                    device_id={axis: peer}, device_id_type=MESH,
                )
                copy.wait_send()
                copy.wait_recv()
            return 0
        lax.fori_loop(1, n, one, 0)

    def ye_do(start):
        spread("gy", me_y, ny, lambda p: ye_send.at[p], lambda p: ye_recv.at[p],
               lambda p: ye_s.at[p], lambda p: ye_r.at[p], start)

    def yp_do(h, start):
        spread("gy", me_y, ny, lambda p: yp_send.at[h, p], lambda p: yp_recv.at[h, p],
               lambda p: yp_s.at[h, p], lambda p: yp_r.at[h, p], start)

    def ya_do(h, start):
        spread("gy", me_y, ny, lambda p: ya_send.at[h, p], lambda p: ya_recv.at[h, p],
               lambda p: ya_s.at[h, p], lambda p: ya_r.at[h, p], start)

    def ze_do(start):
        spread("gz", me_z, nz, lambda p: ze.at[me_z], lambda p: ze.at[p],
               lambda p: ze_s.at[p], lambda p: ze_r.at[p], start)

    def zp_do(h, start):
        spread("gz", me_z, nz, lambda p: zp.at[h, me_z], lambda p: zp.at[h, p],
               lambda p: zp_s.at[h, p], lambda p: zp_r.at[h, p], start)

    inv = [recip(0.5 * NU * jnp.full((8, LANES), diff[k], jnp.float32))[:1] for k in range(phases)]
    slab = (ly, LANES)
    zones, zzeros = jnp.ones(slab, jnp.float32), jnp.zeros(slab, jnp.float32)
    plane = (lz, LANES)
    ones, zeros = jnp.ones(plane, jnp.float32), jnp.zeros(plane, jnp.float32)
    pl.semaphore_wait(barrier, ny + nz - 2)

    halo_y = []
    for h in range(halves):
        cols = pl.ds(h * LANES, LANES)
        for d, (row, place, peer) in enumerate(((ly - 1, 0, up_y), (0, ly + 1, down_y))):
            copy = pltpu.make_async_remote_copy(
                src_ref=u_hbm.at[row, :, cols], dst_ref=u_v[h].at[place],
                send_sem=hy_s.at[h, d], recv_sem=hy_r.at[h, d],
                device_id={"gy": peer}, device_id_type=MESH,
            )
            copy.start()
            halo_y.append(copy)

    for h in range(halves):
        loads[1][h].wait()
        for d, z in ((0, lz - 1), (1, 0)):
            def pick(y, _):
                zh_send[d, h, pl.ds(y, 1), :] = u_v[h][y + 1, pl.ds(z, 1), :]
                return 0
            lax.fori_loop(0, ly, pick, 0, unroll=8)
    halo_z = []
    for d, peer in ((0, up_z), (1, down_z)):
        copy = pltpu.make_async_remote_copy(
            src_ref=zh_send.at[d], dst_ref=zh_recv.at[d],
            send_sem=hz_s.at[d], recv_sem=hz_r.at[d],
            device_id={"gz": peer}, device_id_type=MESH,
        )
        copy.start()
        halo_z.append(copy)

    for h in range(halves):
        loads[0][h].wait()

    def matrix_y(y, carry):
        at = pl.ds(pl.multiple_of(y * lz, lz), lz)
        after = []
        for h in range(halves):
            slack, prod, low, _ = carry[h]
            label = l_v[h][y]
            rate = jnp.broadcast_to(inv[0], plane)
            for k in range(1, phases):
                rate = jnp.where(label == k, inv[k], rate)
            g_v[h][at, :] = rate
            rz[h][pl.ds(y, lz, stride=pitch_z), :] = rate
            slack, ratio = eliminate(slack, rate)
            cy[h][at, :] = ratio
            later = prod * ratio
            after.append((slack, later, low + prod * later, ratio))
        return after

    ends = lax.fori_loop(0, ly, matrix_y, [(ones, ones, zeros, zeros)] * halves)
    for h in range(halves):
        _, prod, low, last = ends[h]
        for j in range(ny):
            part = slice(rp * j, rp * (j + 1))
            ye_send[j, h, 0] = low[part]
            ye_send[j, h, 1] = prod[part]
            ye_send[j, h, 2] = last[part]
    ye_recv[me_y] = ye_send[me_y]
    ye_do(True)

    for h in range(halves):
        def turn_g(b, _):
            block = g_v[h][pl.ds(pl.multiple_of(b * LANES, LANES), LANES), :]
            cx[pl.ds(h * LANES * pitch_x + b, LANES, stride=pitch_x), :] = block.T
            return 0
        lax.fori_loop(0, blocks, turn_g, 0, unroll=4)

    def at_x(i):
        return pl.ds(i * pitch_x, blocks)

    lines = (blocks, LANES)
    lone, lzero = jnp.ones(lines, jnp.float32), jnp.zeros(lines, jnp.float32)

    steps = half_x // blocks

    def matrix_x(b, carry):
        slacks = list(carry)
        places = [[at_x(b * steps + k) for k in range(steps)],
                  [at_x(lx - 1 - b * steps - k) for k in range(steps)]]
        rates = [[cx[at, :] for at in side] for side in places]
        for k in range(steps):
            for side in range(2):
                slacks[side], rates[side][k] = eliminate(slacks[side], rates[side][k])
        for side in range(2):
            for k in range(steps):
                cx[places[side][k], :] = rates[side][k]
        return tuple(slacks)

    for copy in halo_y + halo_z:
        copy.wait()
    for h in range(halves):
        loads[2][h].wait()
        loads[3][h].wait()

        @pl.when(me_y == 0)
        def _():
            u_v[h][0] = zeros

        @pl.when(me_y == ny - 1)
        def _():
            u_v[h][ly + 1] = zeros

        @pl.when(me_z == 0)
        def _():
            zh_recv[0, h] = zzeros

        @pl.when(me_z == nz - 1)
        def _():
            zh_recv[1, h] = zzeros

    sub = lax.broadcasted_iota(jnp.int32, plane, 0)
    lane = lax.broadcasted_iota(jnp.int32, plane, 1)

    def right_x(b, carry):
        carry = matrix_x(b, carry)
        done = [[] for _ in range(halves)]
        for k in range(per_block):
            y = b * per_block + k
            at = pl.ds(pl.multiple_of(y * lz, lz), lz)
            mids = [u_v[h][y + 1] for h in range(halves)]
            ups = [pltpu.roll(m, LANES - 1, 1) for m in mids]
            downs = [pltpu.roll(m, 1, 1) for m in mids]
            for h in range(halves):
                mid = mids[h]
                after = jnp.where(lane == LANES - 1, ups[h + 1] if h + 1 < halves else 0.0, ups[h])
                before = jnp.where(lane == 0, downs[h - 1] if h else 0.0, downs[h])
                twice = 2.0 * mid
                lap_x = after + before - twice
                lap_y = u_v[h][y] + u_v[h][y + 2] - twice
                below = jnp.where(sub == 0, zh_recv[0, h, pl.ds(y, 1), :], pltpu.roll(mid, 1, 0))
                above = jnp.where(
                    sub == lz - 1, zh_recv[1, h, pl.ds(y, 1), :], pltpu.roll(mid, lz - 1, 0)
                )
                lap_z = below + above - twice
                lapz[h][at, :] = lap_z
                source = m_v[h][y].astype(jnp.float32) * s_v[h][y]
                value = g_v[h][at, :] * (mid + source) + (lap_x + 2.0 * (lap_y + lap_z))
                done[h].append(value)
        for h in range(halves):
            block = jnp.concatenate(done[h], 0)
            rt[pl.ds(h * LANES * pitch_x + b, LANES, stride=pitch_x), :] = block.T
        return carry

    slack_one, slack_two = lax.fori_loop(0, blocks, right_x, (lone, lone))
    middle = recip(slack_one + slack_two - slack_one * slack_two)

    def forward_x(i, carry):
        one, two = carry
        low_at, high_at = at_x(i), at_x(lx - 1 - i)
        one = (rt[low_at, :] + one) * cx[low_at, :]
        rt[low_at, :] = one
        two = (rt[high_at, :] + two) * cx[high_at, :]
        rt[high_at, :] = two
        return one, two

    one, two = lax.fori_loop(0, half_x, forward_x, (lzero, lzero), unroll=8)
    low_mid, high_mid = at_x(half_x - 1), at_x(half_x)
    first = (one + cx[low_mid, :] * two) * middle
    second = (two + cx[high_mid, :] * one) * middle
    rt[low_mid, :] = first
    rt[high_mid, :] = second

    def backward_x(i, carry):
        one, two = carry
        low_at, high_at = at_x(half_x - 1 - i), at_x(half_x + i)
        one = rt[low_at, :] + cx[low_at, :] * one
        rt[low_at, :] = one
        two = rt[high_at, :] + cx[high_at, :] * two
        rt[high_at, :] = two
        return one, two

    lax.fori_loop(1, half_x, backward_x, (first, second), unroll=8)

    for h in range(halves):
        def local_y(b, carry):
            value, prod, head = carry
            block = rt[pl.ds(h * LANES * pitch_x + b, LANES, stride=pitch_x), :].T
            for k in range(per_block):
                y = b * per_block + k
                at = pl.ds(pl.multiple_of(y * lz, lz), lz)
                lap_y = u_v[h][y] + u_v[h][y + 2] - 2.0 * u_v[h][y + 1]
                right = g_v[h][at, :] * block[k * lz:(k + 1) * lz] - lap_y
                r2[h][at, :] = right
                ratio = cy[h][at, :]
                value = (right + value) * ratio
                head = head + value * prod
                prod = prod * ratio
            return value, prod, head

        value, _, head = lax.fori_loop(0, blocks, local_y, (zeros, ones, zeros), unroll=2)
        for j in range(ny):
            part = slice(rp * j, rp * (j + 1))
            yp_send[h, j, 0] = head[part]
            yp_send[h, j, 1] = value[part]
        yp_recv[h, me_y] = yp_send[h, me_y]
        yp_do(h, True)

    def pivots(n, coef, keep, shape):
        def one(k, slope):
            low, cross = coef(k, 0), coef(k, 1)
            pivot = recip(1.0 - low * slope)
            keep[k, 0] = slope
            keep[k, 1] = pivot
            keep[k, 2] = pivot * cross
            return coef(k, 2) + cross * cross * slope * pivot

        lax.fori_loop(0, n, one, jnp.zeros(shape, jnp.float32))

    def chain(n, coef, plain, keep, answer, shape):
        none = jnp.zeros(shape, jnp.float32)

        def forward(k, offset):
            head = keep[k, 1] * (plain(k, 0) + coef(k, 0) * offset)
            keep[k, 3] = offset
            keep[k, 4] = head
            return plain(k, 1) + coef(k, 1) * (offset + keep[k, 0] * head)

        lax.fori_loop(0, n, forward, none)

        def backward(i, after):
            k = n - 1 - i
            head = keep[k, 4] + keep[k, 2] * after
            answer(k, keep[k, 3] + keep[k, 0] * head, after)
            return head

        lax.fori_loop(0, n, backward, none)

    def matrix_z(z, carry):
        after = []
        for h in range(halves):
            slack, prod, low, _ = carry[h]
            slack, ratio = eliminate(slack, rz[h][pl.ds(z * pitch_z, ly), :])
            cz[h][z] = ratio
            later = prod * ratio
            after.append((slack, later, low + prod * later, ratio))
        return after

    state_z = [(zones, zones, zzeros, zzeros)] * halves
    state_z = lax.fori_loop(0, lz // 2, matrix_z, state_z)

    ye_do(False)
    for h in range(halves):
        pivots(ny, lambda k, c: ye_recv[k, h, c], ychain.at[h], (rp, LANES))
    for h in range(halves):
        yp_do(h, False)

        def answer_y(k, left, right):
            ya_send[h, k, 0] = left
            ya_send[h, k, 1] = right

        chain(ny, lambda k, c: ye_recv[k, h, c], lambda k, c: yp_recv[h, k, c],
              ychain.at[h], answer_y, (rp, LANES))
        ya_recv[h, me_y] = ya_send[h, me_y]
        ya_do(h, True)

    state_z = lax.fori_loop(lz // 2, lz, matrix_z, state_z)
    for h in range(halves):
        _, prod, low, last = state_z[h]
        ze[me_z, h, 0] = low
        ze[me_z, h, 1] = prod
        ze[me_z, h, 2] = last
    ze_do(True)

    for h in range(halves):
        ya_do(h, False)
        left = jnp.concatenate([ya_recv[h, j, 0] for j in range(ny)], 0)
        right = jnp.concatenate([ya_recv[h, j, 1] for j in range(ny)], 0)

        def forward_y(y, value):
            at = pl.ds(pl.multiple_of(y * lz, lz), lz)
            value = (r2[h][at, :] + value) * cy[h][at, :]
            r2[h][at, :] = value
            return value

        lax.fori_loop(0, ly, forward_y, left, unroll=4)

        def backward_y(i, value):
            y = ly - 1 - i
            at = pl.ds(pl.multiple_of(y * lz, lz), lz)
            value = r2[h][at, :] + cy[h][at, :] * value
            rz[h][pl.ds(y, lz, stride=pitch_z), :] = g_v[h][at, :] * value - lapz[h][at, :]
            return value

        lax.fori_loop(0, ly, backward_y, right, unroll=4)

        def local_z(z, carry):
            value, prod, head = carry
            ratio = cz[h][z]
            value = (rz[h][pl.ds(z * pitch_z, ly), :] + value) * ratio
            return value, prod * ratio, head + value * prod

        value, _, head = lax.fori_loop(0, lz, local_z, (zzeros, zones, zzeros), unroll=4)
        zp[h, me_z, 0] = head
        zp[h, me_z, 1] = value
        zp_do(h, True)

    ze_do(False)
    for h in range(halves):
        pivots(nz, lambda k, c: ze[k, h, c], zchain.at[h], slab)
    for h in range(halves):
        zp_do(h, False)

        def answer_z(k, left, right):
            zchain[h, k, 5] = left
            zchain[h, k, 6] = right

        chain(nz, lambda k, c: ze[k, h, c], lambda k, c: zp[h, k, c],
              zchain.at[h], answer_z, slab)
        left, right = zchain[h, me_z, 5], zchain[h, me_z, 6]

        def forward_z(z, value):
            at = pl.ds(z * pitch_z, ly)
            value = (rz[h][at, :] + value) * cz[h][z]
            rz[h][at, :] = value
            return value

        lax.fori_loop(0, lz, forward_z, left, unroll=4)

        def backward_z(i, value):
            z = lz - 1 - i
            value = rz[h][pl.ds(z * pitch_z, ly), :] + cz[h][z] * value
            rz[h][pl.ds(z * pitch_z, ly), :] = value
            return value

        lax.fori_loop(0, lz, backward_z, right, unroll=4)

        def turn_out(y, _):
            out[y, :, pl.ds(h * LANES, LANES)] = rz[h][pl.ds(y, lz, stride=pitch_z), :]
            return 0

        lax.fori_loop(0, ly, turn_out, 0, unroll=4)


def body(ny, nz, species_field, reaction_source, interface_mask, phase_labels, phase_diffusivity):
    ly, lz, lx = species_field.shape
    halves = lx // LANES
    rows = ly * lz
    blocks = rows // LANES
    rp = lz // ny
    f32 = jnp.float32

    def vm(*shape, dtype=f32):
        return pltpu.VMEM(shape, dtype)

    def pair(*shape, dtype=f32):
        return [vm(*shape, dtype=dtype) for _ in range(halves)]

    def sems(*shape):
        return pltpu.SemaphoreType.DMA(shape)

    scratch = [
        pair(ly + 2, lz, LANES), pair(ly, lz, LANES),
        pair(ly, lz, LANES, dtype=jnp.int32), pair(ly, lz, LANES, dtype=jnp.int32),
        pair(rows, LANES), pair(rows, LANES), pair(lz, ly, LANES), pair(rows, LANES),
        vm(lx * (blocks + 1), LANES), vm(lx * (blocks + 1), LANES),
        pair(rows, LANES), pair(lz * (ly + 1), LANES),
        vm(2, halves, ly, LANES), vm(2, halves, ly, LANES),
        vm(ny, halves, 3, rp, LANES), vm(ny, halves, 3, rp, LANES),
        vm(halves, ny, 2, rp, LANES), vm(halves, ny, 2, rp, LANES),
        vm(halves, ny, 2, rp, LANES), vm(halves, ny, 2, rp, LANES),
        vm(nz, halves, 3, ly, LANES), vm(halves, nz, 2, ly, LANES),
        vm(halves, ny, 5, rp, LANES), vm(halves, nz, 7, ly, LANES),
        sems(4, halves),
        sems(halves, 2), sems(halves, 2), sems(2), sems(2),
        sems(ny), sems(ny), sems(halves, ny), sems(halves, ny), sems(halves, ny), sems(halves, ny),
        sems(nz), sems(nz), sems(halves, nz), sems(halves, nz),
    ]
    anywhere = pl.BlockSpec(memory_space=pl.ANY)
    return pl.pallas_call(
        functools.partial(kernel, ny, nz, ly, lz, lx, phase_diffusivity.shape[0]),
        out_shape=pltpu.VMEM(species_field.shape, f32),
        in_specs=[pl.BlockSpec(memory_space=pltpu.SMEM)] + [anywhere] * 4,
        out_specs=pl.BlockSpec(memory_space=pltpu.VMEM),
        scratch_shapes=scratch,
        compiler_params=pltpu.CompilerParams(
            collective_id=0, has_side_effects=True, vmem_limit_bytes=56 * 1024 * 1024
        ),
    )(phase_diffusivity, species_field, reaction_source, interface_mask, phase_labels)


def solution(mesh):
    spec = P("gy", "gz", None)
    return jax.shard_map(
        functools.partial(body, mesh.shape["gy"], mesh.shape["gz"]),
        mesh=mesh, in_specs=(spec,) * 4 + (P(),), out_specs=spec, check_vma=False,
    )
```

```python
import functools

import jax
import jax.numpy as jnp
from jax import lax
from jax.experimental import pallas as pl
from jax.experimental.pallas import tpu as pltpu
from jax.sharding import PartitionSpec as P

NU = 400
LANES = 128
MESH = pl.DeviceIdType.MESH


def recip(value):
    return pl.reciprocal(value, approx=False)


def eliminate(slack, rate):
    excess = rate + slack
    ratio = recip(1.0 + excess)
    return excess * ratio, ratio


def kernel(
    ny, nz, ly, lz, lx, phases,
    diff, u_hbm, s_hbm, m_hbm, l_hbm, out,
    u_v, s_v, m_v, l_v, g_v, cy, cz, lapz, rt, cx, r2, rz,
    zh_send, zh_recv, ye_send, ye_recv, yp_send, yp_recv, ya_send, ya_recv, ze, zp,
    ychain, zchain,
    loc_sem, hy_s, hy_r, hz_s, hz_r, ye_s, ye_r, yp_s, yp_r, ya_s, ya_r,
    ze_s, ze_r, zp_s, zp_r,
):
    halves = lx // LANES
    rows = ly * lz
    blocks = rows // LANES
    per_block = LANES // lz
    rp = lz // ny
    half_x = lx // 2
    pitch_x, pitch_z = blocks + 1, ly + 1
    me_y = lax.axis_index("gy")
    me_z = lax.axis_index("gz")
    up_y, down_y = lax.rem(me_y + 1, ny), lax.rem(me_y + ny - 1, ny)
    up_z, down_z = lax.rem(me_z + 1, nz), lax.rem(me_z + nz - 1, nz)

    loads = []
    for index, (src, dst) in enumerate(((l_hbm, l_v), (u_hbm, u_v), (s_hbm, s_v), (m_hbm, m_v))):
        pair = []
        for h in range(halves):
            target = dst[h].at[pl.ds(1, ly)] if dst is u_v else dst[h]
            copy = pltpu.make_async_copy(
                src.at[:, :, pl.ds(h * LANES, LANES)], target, loc_sem.at[index, h]
            )
            copy.start()
            pair.append(copy)
        loads.append(pair)

    barrier = pltpu.get_barrier_semaphore()

    def greet(axis, me, n):
        def one(o, _):
            pl.semaphore_signal(
                barrier, inc=1, device_id={axis: lax.rem(me + o, n)}, device_id_type=MESH
            )
            return 0
        lax.fori_loop(1, n, one, 0)

    greet("gy", me_y, ny)
    greet("gz", me_z, nz)
    def spread(axis, me, n, source, target, send, recv, start):
        def one(o, _):
            peer = lax.rem(me + o, n)
            if start:
                pltpu.make_async_remote_copy(
                    src_ref=source(peer), dst_ref=target(me),
                    send_sem=send(peer), recv_sem=recv(me),
                    device_id={axis: peer}, device_id_type=MESH,
                ).start()
            else:
                copy = pltpu.make_async_remote_copy(
                    src_ref=source(peer), dst_ref=target(peer),
                    send_sem=send(peer), recv_sem=recv(peer),
                    device_id={axis: peer}, device_id_type=MESH,
                )
                copy.wait_send()
                copy.wait_recv()
            return 0
        lax.fori_loop(1, n, one, 0)

    def ye_do(start):
        spread("gy", me_y, ny, lambda p: ye_send.at[p], lambda p: ye_recv.at[p],
               lambda p: ye_s.at[p], lambda p: ye_r.at[p], start)

    def yp_do(h, start):
        spread("gy", me_y, ny, lambda p: yp_send.at[h, p], lambda p: yp_recv.at[h, p],
               lambda p: yp_s.at[h, p], lambda p: yp_r.at[h, p], start)

    def ya_do(h, start):
        spread("gy", me_y, ny, lambda p: ya_send.at[h, p], lambda p: ya_recv.at[h, p],
               lambda p: ya_s.at[h, p], lambda p: ya_r.at[h, p], start)

    def ze_do(start):
        spread("gz", me_z, nz, lambda p: ze.at[me_z], lambda p: ze.at[p],
               lambda p: ze_s.at[p], lambda p: ze_r.at[p], start)

    def zp_do(h, start):
        spread("gz", me_z, nz, lambda p: zp.at[h, me_z], lambda p: zp.at[h, p],
               lambda p: zp_s.at[h, p], lambda p: zp_r.at[h, p], start)

    inv = [recip(0.5 * NU * jnp.full((8, LANES), diff[k], jnp.float32))[:1] for k in range(phases)]
    slab = (ly, LANES)
    zones, zzeros = jnp.ones(slab, jnp.float32), jnp.zeros(slab, jnp.float32)
    plane = (lz, LANES)
    ones, zeros = jnp.ones(plane, jnp.float32), jnp.zeros(plane, jnp.float32)
    pl.semaphore_wait(barrier, ny + nz - 2)

    halo_y = []
    for h in range(halves):
        cols = pl.ds(h * LANES, LANES)
        for d, (row, place, peer) in enumerate(((ly - 1, 0, up_y), (0, ly + 1, down_y))):
            copy = pltpu.make_async_remote_copy(
                src_ref=u_hbm.at[row, :, cols], dst_ref=u_v[h].at[place],
                send_sem=hy_s.at[h, d], recv_sem=hy_r.at[h, d],
                device_id={"gy": peer}, device_id_type=MESH,
            )
            copy.start()
            halo_y.append(copy)

    for h in range(halves):
        loads[1][h].wait()
        for d, z in ((0, lz - 1), (1, 0)):
            def pick(y, _):
                zh_send[d, h, pl.ds(y, 1), :] = u_v[h][y + 1, pl.ds(z, 1), :]
                return 0
            lax.fori_loop(0, ly, pick, 0, unroll=8)
    halo_z = []
    for d, peer in ((0, up_z), (1, down_z)):
        copy = pltpu.make_async_remote_copy(
            src_ref=zh_send.at[d], dst_ref=zh_recv.at[d],
            send_sem=hz_s.at[d], recv_sem=hz_r.at[d],
            device_id={"gz": peer}, device_id_type=MESH,
        )
        copy.start()
        halo_z.append(copy)

    for h in range(halves):
        loads[0][h].wait()

    def matrix_y(y, carry):
        at = pl.ds(pl.multiple_of(y * lz, lz), lz)
        after = []
        for h in range(halves):
            slack, prod, low, _ = carry[h]
            label = l_v[h][y]
            rate = jnp.broadcast_to(inv[0], plane)
            for k in range(1, phases):
                rate = jnp.where(label == k, inv[k], rate)
            g_v[h][at, :] = rate
            rz[h][pl.ds(y, lz, stride=pitch_z), :] = rate
            slack, ratio = eliminate(slack, rate)
            cy[h][at, :] = ratio
            later = prod * ratio
            after.append((slack, later, low + prod * later, ratio))
        return after

    ends = lax.fori_loop(0, ly, matrix_y, [(ones, ones, zeros, zeros)] * halves)
    for h in range(halves):
        _, prod, low, last = ends[h]
        for j in range(ny):
            part = slice(rp * j, rp * (j + 1))
            ye_send[j, h, 0] = low[part]
            ye_send[j, h, 1] = prod[part]
            ye_send[j, h, 2] = last[part]
    ye_recv[me_y] = ye_send[me_y]
    ye_do(True)

    for h in range(halves):
        def turn_g(b, _):
            block = g_v[h][pl.ds(pl.multiple_of(b * LANES, LANES), LANES), :]
            cx[pl.ds(h * LANES * pitch_x + b, LANES, stride=pitch_x), :] = block.T
            return 0
        lax.fori_loop(0, blocks, turn_g, 0, unroll=8)

    def at_x(i):
        return pl.ds(i * pitch_x, blocks)

    lines = (blocks, LANES)
    lone, lzero = jnp.ones(lines, jnp.float32), jnp.zeros(lines, jnp.float32)

    steps = half_x // blocks

    def matrix_x(b, carry):
        slacks = list(carry)
        places = [[at_x(b * steps + k) for k in range(steps)],
                  [at_x(lx - 1 - b * steps - k) for k in range(steps)]]
        rates = [[cx[at, :] for at in side] for side in places]
        for k in range(steps):
            for side in range(2):
                slacks[side], rates[side][k] = eliminate(slacks[side], rates[side][k])
        for side in range(2):
            for k in range(steps):
                cx[places[side][k], :] = rates[side][k]
        return tuple(slacks)

    for copy in halo_y + halo_z:
        copy.wait()
    for h in range(halves):
        loads[2][h].wait()
        loads[3][h].wait()

        @pl.when(me_y == 0)
        def _():
            u_v[h][0] = zeros

        @pl.when(me_y == ny - 1)
        def _():
            u_v[h][ly + 1] = zeros

        @pl.when(me_z == 0)
        def _():
            zh_recv[0, h] = zzeros

        @pl.when(me_z == nz - 1)
        def _():
            zh_recv[1, h] = zzeros

    sub = lax.broadcasted_iota(jnp.int32, plane, 0)
    lane = lax.broadcasted_iota(jnp.int32, plane, 1)

    def right_x(b, carry):
        carry = matrix_x(b, carry)
        done = [[] for _ in range(halves)]
        for k in range(per_block):
            y = b * per_block + k
            at = pl.ds(pl.multiple_of(y * lz, lz), lz)
            mids = [u_v[h][y + 1] for h in range(halves)]
            ups = [pltpu.roll(m, LANES - 1, 1) for m in mids]
            downs = [pltpu.roll(m, 1, 1) for m in mids]
            for h in range(halves):
                mid = mids[h]
                after = jnp.where(lane == LANES - 1, ups[h + 1] if h + 1 < halves else 0.0, ups[h])
                before = jnp.where(lane == 0, downs[h - 1] if h else 0.0, downs[h])
                twice = 2.0 * mid
                lap_x = after + before - twice
                lap_y = u_v[h][y] + u_v[h][y + 2] - twice
                below = jnp.where(sub == 0, zh_recv[0, h, pl.ds(y, 1), :], pltpu.roll(mid, 1, 0))
                above = jnp.where(
                    sub == lz - 1, zh_recv[1, h, pl.ds(y, 1), :], pltpu.roll(mid, lz - 1, 0)
                )
                lap_z = below + above - twice
                lapz[h][at, :] = lap_z
                source = m_v[h][y].astype(jnp.float32) * s_v[h][y]
                value = g_v[h][at, :] * (mid + source) + (lap_x + 2.0 * (lap_y + lap_z))
                done[h].append(value)
        for h in range(halves):
            block = jnp.concatenate(done[h], 0)
            rt[pl.ds(h * LANES * pitch_x + b, LANES, stride=pitch_x), :] = block.T
        return carry

    slack_one, slack_two = lax.fori_loop(0, blocks, right_x, (lone, lone), unroll=2)
    middle = recip(slack_one + slack_two - slack_one * slack_two)

    def forward_x(i, carry):
        one, two = carry
        low_at, high_at = at_x(i), at_x(lx - 1 - i)
        one = (rt[low_at, :] + one) * cx[low_at, :]
        rt[low_at, :] = one
        two = (rt[high_at, :] + two) * cx[high_at, :]
        rt[high_at, :] = two
        return one, two

    one, two = lax.fori_loop(0, half_x, forward_x, (lzero, lzero), unroll=8)
    low_mid, high_mid = at_x(half_x - 1), at_x(half_x)
    first = (one + cx[low_mid, :] * two) * middle
    second = (two + cx[high_mid, :] * one) * middle
    rt[low_mid, :] = first
    rt[high_mid, :] = second

    def backward_x(i, carry):
        one, two = carry
        low_at, high_at = at_x(half_x - 1 - i), at_x(half_x + i)
        one = rt[low_at, :] + cx[low_at, :] * one
        rt[low_at, :] = one
        two = rt[high_at, :] + cx[high_at, :] * two
        rt[high_at, :] = two
        return one, two

    lax.fori_loop(1, half_x, backward_x, (first, second), unroll=8)

    for h in range(halves):
        def local_y(b, carry):
            value, prod, head = carry
            block = rt[pl.ds(h * LANES * pitch_x + b, LANES, stride=pitch_x), :].T
            for k in range(per_block):
                y = b * per_block + k
                at = pl.ds(pl.multiple_of(y * lz, lz), lz)
                lap_y = u_v[h][y] + u_v[h][y + 2] - 2.0 * u_v[h][y + 1]
                right = g_v[h][at, :] * block[k * lz:(k + 1) * lz] - lap_y
                r2[h][at, :] = right
                ratio = cy[h][at, :]
                value = (right + value) * ratio
                head = head + value * prod
                prod = prod * ratio
            return value, prod, head

        value, _, head = lax.fori_loop(0, blocks, local_y, (zeros, ones, zeros), unroll=4)
        for j in range(ny):
            part = slice(rp * j, rp * (j + 1))
            yp_send[h, j, 0] = head[part]
            yp_send[h, j, 1] = value[part]
        yp_recv[h, me_y] = yp_send[h, me_y]
        yp_do(h, True)

    def pivots(n, coef, keep, shape):
        def one(k, slope):
            low, cross = coef(k, 0), coef(k, 1)
            pivot = recip(1.0 - low * slope)
            keep[k, 0] = slope
            keep[k, 1] = pivot
            keep[k, 2] = pivot * cross
            return coef(k, 2) + cross * cross * slope * pivot

        lax.fori_loop(0, n, one, jnp.zeros(shape, jnp.float32))

    def chain(n, coef, plain, keep, answer, shape):
        none = jnp.zeros(shape, jnp.float32)

        def forward(k, offset):
            head = keep[k, 1] * (plain(k, 0) + coef(k, 0) * offset)
            keep[k, 3] = offset
            keep[k, 4] = head
            return plain(k, 1) + coef(k, 1) * (offset + keep[k, 0] * head)

        lax.fori_loop(0, n, forward, none)

        def backward(i, after):
            k = n - 1 - i
            head = keep[k, 4] + keep[k, 2] * after
            answer(k, keep[k, 3] + keep[k, 0] * head, after)
            return head

        lax.fori_loop(0, n, backward, none)

    def matrix_z(z, carry):
        after = []
        for h in range(halves):
            slack, prod, low, _ = carry[h]
            slack, ratio = eliminate(slack, rz[h][pl.ds(z * pitch_z, ly), :])
            cz[h][z] = ratio
            later = prod * ratio
            after.append((slack, later, low + prod * later, ratio))
        return after

    state_z = [(zones, zones, zzeros, zzeros)] * halves
    state_z = lax.fori_loop(0, lz // 2, matrix_z, state_z)

    ye_do(False)
    for h in range(halves):
        pivots(ny, lambda k, c: ye_recv[k, h, c], ychain.at[h], (rp, LANES))
    for h in range(halves):
        yp_do(h, False)

        def answer_y(k, left, right):
            ya_send[h, k, 0] = left
            ya_send[h, k, 1] = right

        chain(ny, lambda k, c: ye_recv[k, h, c], lambda k, c: yp_recv[h, k, c],
              ychain.at[h], answer_y, (rp, LANES))
        ya_recv[h, me_y] = ya_send[h, me_y]
        ya_do(h, True)

    state_z = lax.fori_loop(lz // 2, lz, matrix_z, state_z)
    for h in range(halves):
        _, prod, low, last = state_z[h]
        ze[me_z, h, 0] = low
        ze[me_z, h, 1] = prod
        ze[me_z, h, 2] = last
    ze_do(True)

    for h in range(halves):
        ya_do(h, False)
        left = jnp.concatenate([ya_recv[h, j, 0] for j in range(ny)], 0)
        right = jnp.concatenate([ya_recv[h, j, 1] for j in range(ny)], 0)

        def forward_y(y, value):
            at = pl.ds(pl.multiple_of(y * lz, lz), lz)
            value = (r2[h][at, :] + value) * cy[h][at, :]
            r2[h][at, :] = value
            return value

        lax.fori_loop(0, ly, forward_y, left, unroll=4)

        def backward_y(i, value):
            y = ly - 1 - i
            at = pl.ds(pl.multiple_of(y * lz, lz), lz)
            value = r2[h][at, :] + cy[h][at, :] * value
            rz[h][pl.ds(y, lz, stride=pitch_z), :] = g_v[h][at, :] * value - lapz[h][at, :]
            return value

        lax.fori_loop(0, ly, backward_y, right, unroll=4)

        def local_z(z, carry):
            value, prod, head = carry
            ratio = cz[h][z]
            value = (rz[h][pl.ds(z * pitch_z, ly), :] + value) * ratio
            return value, prod * ratio, head + value * prod

        value, _, head = lax.fori_loop(0, lz, local_z, (zzeros, zones, zzeros), unroll=4)
        zp[h, me_z, 0] = head
        zp[h, me_z, 1] = value
        zp_do(h, True)

    ze_do(False)
    for h in range(halves):
        pivots(nz, lambda k, c: ze[k, h, c], zchain.at[h], slab)
    for h in range(halves):
        zp_do(h, False)

        def answer_z(k, left, right):
            zchain[h, k, 5] = left
            zchain[h, k, 6] = right

        chain(nz, lambda k, c: ze[k, h, c], lambda k, c: zp[h, k, c],
              zchain.at[h], answer_z, slab)
        left, right = zchain[h, me_z, 5], zchain[h, me_z, 6]

        def forward_z(z, value):
            at = pl.ds(z * pitch_z, ly)
            value = (rz[h][at, :] + value) * cz[h][z]
            rz[h][at, :] = value
            return value

        lax.fori_loop(0, lz, forward_z, left, unroll=4)

        def backward_z(i, value):
            z = lz - 1 - i
            value = rz[h][pl.ds(z * pitch_z, ly), :] + cz[h][z] * value
            rz[h][pl.ds(z * pitch_z, ly), :] = value
            return value

        lax.fori_loop(0, lz, backward_z, right, unroll=4)

        def turn_out(y, _):
            out[y, :, pl.ds(h * LANES, LANES)] = rz[h][pl.ds(y, lz, stride=pitch_z), :]
            return 0

        lax.fori_loop(0, ly, turn_out, 0, unroll=4)


def body(ny, nz, species_field, reaction_source, interface_mask, phase_labels, phase_diffusivity):
    ly, lz, lx = species_field.shape
    halves = lx // LANES
    rows = ly * lz
    blocks = rows // LANES
    rp = lz // ny
    f32 = jnp.float32

    def vm(*shape, dtype=f32):
        return pltpu.VMEM(shape, dtype)

    def pair(*shape, dtype=f32):
        return [vm(*shape, dtype=dtype) for _ in range(halves)]

    def sems(*shape):
        return pltpu.SemaphoreType.DMA(shape)

    scratch = [
        pair(ly + 2, lz, LANES), pair(ly, lz, LANES),
        pair(ly, lz, LANES, dtype=jnp.int32), pair(ly, lz, LANES, dtype=jnp.int32),
        pair(rows, LANES), pair(rows, LANES), pair(lz, ly, LANES), pair(rows, LANES),
        vm(lx * (blocks + 1), LANES), vm(lx * (blocks + 1), LANES),
        pair(rows, LANES), pair(lz * (ly + 1), LANES),
        vm(2, halves, ly, LANES), vm(2, halves, ly, LANES),
        vm(ny, halves, 3, rp, LANES), vm(ny, halves, 3, rp, LANES),
        vm(halves, ny, 2, rp, LANES), vm(halves, ny, 2, rp, LANES),
        vm(halves, ny, 2, rp, LANES), vm(halves, ny, 2, rp, LANES),
        vm(nz, halves, 3, ly, LANES), vm(halves, nz, 2, ly, LANES),
        vm(halves, ny, 5, rp, LANES), vm(halves, nz, 7, ly, LANES),
        sems(4, halves),
        sems(halves, 2), sems(halves, 2), sems(2), sems(2),
        sems(ny), sems(ny), sems(halves, ny), sems(halves, ny), sems(halves, ny), sems(halves, ny),
        sems(nz), sems(nz), sems(halves, nz), sems(halves, nz),
    ]
    anywhere = pl.BlockSpec(memory_space=pl.ANY)
    return pl.pallas_call(
        functools.partial(kernel, ny, nz, ly, lz, lx, phase_diffusivity.shape[0]),
        out_shape=pltpu.VMEM(species_field.shape, f32),
        in_specs=[pl.BlockSpec(memory_space=pltpu.SMEM)] + [anywhere] * 4,
        out_specs=pl.BlockSpec(memory_space=pltpu.VMEM),
        scratch_shapes=scratch,
        compiler_params=pltpu.CompilerParams(
            collective_id=0, has_side_effects=True, vmem_limit_bytes=56 * 1024 * 1024
        ),
    )(phase_diffusivity, species_field, reaction_source, interface_mask, phase_labels)


def solution(mesh):
    spec = P("gy", "gz", None)
    return jax.shard_map(
        functools.partial(body, mesh.shape["gy"], mesh.shape["gz"]),
        mesh=mesh, in_specs=(spec,) * 4 + (P(),), out_specs=spec, check_vma=False,
    )
```
